256 devices in a mesh: dp: 2 (over core), seq: 8 (over x, y_hi), tensor: 16 (over y_lo, z).
Axes of the slice: x: 4, y: 4 (y_hi: 2, y_lo: 2; y = y_hi * 2 + y_lo), z: 8, core: 2. Of those that a mesh axis runs over, the one named last changes fastest.
Arguments:
- hidden: bfloat16 [512, 5376], P(('dp', 'seq')), may hold values from -16 to 16
- weight: bfloat16 [131072, 5376], P(('seq', 'tensor'), 'dp'), may hold values from -6 to 6
- targets: int32 [512], replicated, may hold values from 0 to 131071
- streams: int32 [512], replicated, may hold values from 0 to 7
- loss_token_mask: int32 [512], replicated, may hold values 0 or 1
- counts: int32 [8], replicated, may hold values from 256 to 2047
- stream_weight: float32 [8], replicated, may hold values from 256 to 2048
Outputs:
- grad_hidden: bfloat16 [512, 5376], P(('dp', 'seq'), 'tensor')
- grad_weight: bfloat16 [131072, 5376], P(('seq', 'tensor'), 'dp')
- token_loss: float32 [512], P(('dp', 'seq'))
The draws below stay inside these ranges and needn't reach their ends.
All inputs are finite; a program needn't handle non-finite values.
Results may differ from the reference program's by a relative error of at most 0.0047.
Values may be sent and summed in bfloat16 or wider, within the bound.
A program may use at most 128 MiB of HBM per device.

```python
import math
import jax
import jax.numpy as jnp
import numpy as np
from jax import lax

D = 5376
STREAMS = 8
TOKENS = 512
VOCAB = 131072


def draw_hidden(key, part):
    key = jax.random.fold_in(key, 5)
    key_scale, key_base = jax.random.split(key, 2)
    row_scale = jnp.exp(jax.random.uniform(key_scale, (TOKENS, 1), minval=0.0, maxval=math.log(3.16)))
    values = row_scale * jnp.clip(jax.random.normal(key_base, (TOKENS, D)), -4.0, 4.0)
    return values.astype(jnp.bfloat16)


def draw_weight(key, part):
    key = jax.random.fold_in(key, 9)
    key_scale, key_base = jax.random.split(key, 2)
    vocab_index = jnp.arange(VOCAB, dtype=jnp.int32)[:, None]
    rising = 1.0 + 2.0 * vocab_index.astype(jnp.float32) / VOCAB
    row_scale = 0.3 * rising * jnp.exp(jax.random.uniform(key_scale, (VOCAB, 1), minval=0.0, maxval=math.log(10.0)))
    base = jnp.clip(jax.random.normal(key_base, (VOCAB, D)), -4.0, 4.0)
    values = row_scale * base / math.sqrt(D)
    return values.astype(jnp.bfloat16)


def touch_ends(values, rng, low, largest):
    place = [jax.random.randint(jax.random.fold_in(rng, axis), (), 0, length) for axis, length in enumerate(values.shape)]
    longest = values.shape.index(max(values.shape))
    next_to = place[:longest] + [(place[longest] + 1) % values.shape[longest]] + place[longest + 1:]
    return values.at[tuple(place)].set(low).at[tuple(next_to)].set(largest)


def wide_ids(key, dims, count, slope):
    weights = [min(1 << octave, count + 1 - (1 << octave)) * (1 << 20) // math.isqrt((1 << octave) ** slope) + 1 for octave in range((count + 1).bit_length()) if 1 << octave <= count]
    deviation = 1 + sum(weights) // (1 << 30)
    grid = np.cumsum(np.array([max(1, weight // deviation) for weight in weights]))
    ticket = jax.random.randint(jax.random.fold_in(key, 1), dims, 0, int(grid[len(weights) - 1]))
    start = jnp.left_shift(1, jnp.searchsorted(jnp.asarray(grid, jnp.int32), ticket, side="right").astype(jnp.int32))
    rank = start - 1 + jax.random.randint(jax.random.fold_in(key, 4), dims, 0, 1 << 30) % jnp.minimum(start, count + 1 - start)
    return jax.random.permutation(jax.random.fold_in(key, 2), count)[rank].astype(jnp.int32)


def setup_inputs(seed: int = 0) -> dict:
    keys = jax.random.split(jax.random.key(seed), 8)
    return {
        "hidden": draw_hidden(jax.random.fold_in(keys[7], 71), 0),
        "weight": draw_weight(jax.random.fold_in(keys[7], 71), 0),
        "targets": touch_ends(wide_ids(keys[2], (TOKENS,), VOCAB, 1), jax.random.fold_in(keys[2], 3), 0, VOCAB - 1).astype(jnp.int32),
        "streams": touch_ends(jax.random.randint(keys[3], (TOKENS,), 0, STREAMS), jax.random.fold_in(keys[3], 1), 0, STREAMS - 1).astype(jnp.int32),
        "loss_token_mask": touch_ends((jax.random.randint(keys[4], (TOKENS,), 0, 4) < 3).astype(jnp.int32), jax.random.fold_in(keys[4], 1), 0, 1),
        "counts": touch_ends(jax.random.randint(keys[5], (STREAMS,), 256, 2048), jax.random.fold_in(keys[5], 1), 256, 2047).astype(jnp.int32),
        "stream_weight": jnp.clip(jnp.exp(jax.random.uniform(keys[6], (STREAMS,), jnp.float32, math.log(256.0), math.log(2048.0))), 256.0, 2048.0),
    }


def reference(hidden, weight, targets, streams, loss_token_mask, counts, stream_weight):
    logits = jnp.dot(hidden, weight.T, preferred_element_type=jnp.float32)
    row_max = jnp.max(logits, axis=1)
    shifted = jnp.exp(logits - row_max[:, None])
    row_total = jnp.sum(shifted, axis=1)
    vocab_ids = lax.broadcasted_iota(jnp.int32, (1, VOCAB), 1)
    target_hit = targets[:, None] == vocab_ids
    target_logit = jnp.sum(jnp.where(target_hit, logits, 0.0), axis=1)
    probabilities = shifted / row_total[:, None]
    stream_fraction = stream_weight / counts.astype(jnp.float32)
    stream_onehot = streams[:, None] == lax.broadcasted_iota(jnp.int32, (1, STREAMS), 1)
    mask_float = loss_token_mask.astype(jnp.float32)
    token_scale = mask_float * jnp.sum(jnp.where(stream_onehot, stream_fraction[None, :], 0.0), axis=1)
    token_loss = mask_float * (row_max + jnp.log(row_total) - target_logit)
    logit_gradients = (token_scale[:, None] * (probabilities - target_hit.astype(jnp.float32))).astype(jnp.bfloat16)
    grad_hidden = jnp.dot(logit_gradients, weight, preferred_element_type=jnp.float32).astype(jnp.bfloat16)
    grad_weight = jnp.dot(logit_gradients.T, hidden, preferred_element_type=jnp.float32).astype(jnp.bfloat16)
    return grad_hidden, grad_weight, token_loss
```

```python
import functools

import jax
import jax.numpy as jnp
from jax import lax
from jax.experimental import pallas as pl
from jax.experimental.pallas import tpu as pltpu
from jax.sharding import PartitionSpec as P

MESH = pl.DeviceIdType.MESH
F32, BF16 = jnp.float32, jnp.bfloat16
V, D, HALF = 1024, 5376, 2688
WA = 1280
WB = HALF - WA
FW = 336
NN = (((1,), (0,)), ((), ()))
NT = (((1,), (1,)), ((), ()))


def device(x, y, z, c):
    return (c, x * 2 + y // 2, (y % 2) * 8 + z)


def aligned(index, unit):
    return pl.multiple_of(index * unit, unit)


def landed(ref, sem):
    pltpu.make_async_copy(ref, ref, sem).wait()


def merge(tiles):
    top = functools.reduce(jnp.maximum, [t[0:1] for t in tiles])
    total = sum(t[1:2] * jnp.exp(t[0:1] - top) for t in tiles)
    target = sum(t[2:3] for t in tiles)
    return top, total, target


def kernel(
    hid, w, tgt, strm, msk, cnt, sw,
    gh, gw, loss,
    wv, hf, part, recv, st_x, st_y, st_z, gt, g, p, gws, lossbuf,
    xa, ya_src, ya, yb, xb_src, xb, fin, zs, zr,
    sem_w, sem_out, sem_send, sem_own, sem_x, sem_f, sem_c, sem_p, sem_l, sem_st, sem_g,
    sem_xa, sem_ya, sem_yb, sem_xb, sem_z,
):
    c, s, t = lax.axis_index("dp"), lax.axis_index("seq"), lax.axis_index("tensor")
    x, yh, yl, z = s // 2, s % 2, t // 8, t % 8
    y = yh * 2 + yl
    sib = device(x, y, z, 1 - c)
    xo = lambda o: (x + o) % 4
    yo = lambda o: (y + o) % 4
    zo = lambda o: (z + o) % 8
    cross, partner = device(x, 3 - y, z, c), device(x, yh * 2 + 1 - yl, z, c)
    sends = []

    def send(src, dst, rsem, dev, unless=None):
        cp = pltpu.make_async_remote_copy(
            src_ref=src, dst_ref=dst, send_sem=sem_send.at[len(sends)], recv_sem=rsem,
            device_id=dev, device_id_type=MESH,
        )
        sends.append((cp, unless))
        if unless is None:
            cp.start()
        else:
            pl.when(jnp.logical_not(unless))(cp.start)

    wcopy = pltpu.make_async_copy(w, wv, sem_w)
    wcopy.start()

    barrier = pltpu.get_barrier_semaphore()
    peers = [sib] + [device(x, y, zo(o), c) for o in range(1, 8)]
    for o in range(1, 4):
        for cc in range(2):
            peers += [device(xo(o), y, z, cc), device(x, yo(o), z, cc)]
    for peer in peers:
        pl.semaphore_signal(barrier, inc=1, device_id=peer, device_id_type=MESH)
    pl.semaphore_wait(barrier, len(peers))

    def blk(k, bx, by, r0=0, n=32):
        return hf.at[k, pl.ds(pl.multiple_of((bx * 2 + by) * 32 + r0, 16), n), :]


    def gather_start(k):
        here = blk(k, x, yh)
        own = pltpu.make_async_copy(hid.at[:, pl.ds(k * HALF, HALF)], here, sem_own.at[k])
        pl.when(c == k)(own.start)
        for o in (1, 3):
            for cc in range(2):
                send(hid.at[:, pl.ds(cc * HALF, HALF)], here, sem_x.at[k, o // 2],
                     device(xo(o), y, z, cc), c != k)
        send(hid.at[:, pl.ds((1 - k) * HALF, HALF)], here, sem_own.at[k], sib, c != k)

    def cross_send(k, j, bx):
        r0 = (1 - yl) * 16
        send(blk(k, bx, yh, r0, 16), blk(k, bx, yh, r0, 16), sem_c.at[k, j], cross)

    def gather_x(k):
        landed(blk(k, x, yh), sem_own.at[k])
        cross_send(k, 0, x)
        landed(blk(k, xo(3), yh), sem_x.at[k, 0])
        send(blk(k, xo(3), yh, 0, 16), blk(k, xo(3), yh, 0, 16), sem_f.at[k, 0],
             device(xo(1), y, z, c))
        landed(blk(k, xo(1), yh), sem_x.at[k, 1])
        send(blk(k, xo(1), yh, 16, 16), blk(k, xo(1), yh, 16, 16), sem_f.at[k, 1],
             device(xo(3), y, z, c))
        cross_send(k, 1, xo(3))
        cross_send(k, 2, xo(1))

    def partner_send(k, j, bx):
        r0 = yl * 16
        ref = blk(k, bx, 1 - yh, r0, 16)
        landed(ref, sem_c.at[k, j])
        send(ref, ref, sem_p.at[k, j], partner)

    def gather_y(k):
        partner_send(k, 0, x)
        landed(blk(k, xo(2), yh, 0, 16), sem_f.at[k, 0])
        landed(blk(k, xo(2), yh, 16, 16), sem_f.at[k, 1])
        cross_send(k, 3, xo(2))
        partner_send(k, 1, xo(3))
        partner_send(k, 2, xo(1))

    def gather_end(k):
        partner_send(k, 3, xo(2))
        r0 = (1 - yl) * 16
        for j, o in enumerate((0, 3, 1, 2)):
            landed(blk(k, xo(o), 1 - yh, r0, 16), sem_p.at[k, j])

    def logits(k):
        def tile(i, _):
            rows = pl.ds(aligned(i, 256), 256)
            full = lax.dot_general(wv[rows, :], hf[k], NT, preferred_element_type=F32)
            part[k, 0, rows, :] = full[:, :128]
            part[k, 1, rows, :] = full[:, 128:]
            return 0

        lax.fori_loop(0, 4, tile, 0)
        send(part.at[k, 1 - c], recv.at[k], sem_l.at[k], sib)

    def row(ref, k):
        return ref[pl.ds(2 * k + c, 1), :]

    def vocab_hit(k, i):
        ids = (s * 16 + t) * V + i * 256 + lax.broadcasted_iota(jnp.int32, (256, 128), 0)
        return ids == row(tgt, k)

    def local_stats(k):
        landed(recv.at[k], sem_l.at[k])

        def add(i, top):
            rows = pl.ds(aligned(i, 256), 256)
            both = part[k, c, rows, :] + recv[k, rows, :]
            recv[k, rows, :] = both
            return jnp.maximum(top, jnp.max(both, axis=0, keepdims=True))

        top = lax.fori_loop(0, 4, add, jnp.full((1, 128), -jnp.inf, F32))

        def expo(i, carry):
            total, target = carry
            rows = pl.ds(aligned(i, 256), 256)
            both = recv[k, rows, :]
            e = jnp.exp(both - top)
            recv[k, rows, :] = e
            target += jnp.sum(jnp.where(vocab_hit(k, i), both, 0.0), axis=0, keepdims=True)
            return total + jnp.sum(e, axis=0, keepdims=True), target

        zero = jnp.zeros((1, 128), F32)
        total, target = lax.fori_loop(0, 4, expo, (zero, zero))
        return top, total, target

    def put(ref, vals):
        ref[...] = jnp.concatenate([*vals, jnp.zeros((5, 128), F32)], axis=0)

    def stats_start(k, buf, vals, me, n, base, dev):
        put(buf.at[k, 0], vals)
        for o in range(1, n):
            send(buf.at[k, 0], buf.at[k, o], sem_st.at[k, base + o], dev(o))

    def stats_end(k, buf, n, base):
        for o in range(1, n):
            landed(buf.at[k, o], sem_st.at[k, base + o])
        return merge([buf[k, o] for o in range(n)])

    def stats_x(k, vals):
        stats_start(k, st_x, vals, x, 4, 0, lambda o: device(xo(o), y, z, c))

    def stats_y(k):
        vals = stats_end(k, st_x, 4, 0)
        stats_start(k, st_y, vals, y, 4, 4, lambda o: device(x, yo(o), z, c))

    def stats_z(k):
        vals = stats_end(k, st_y, 4, 4)
        stats_start(k, st_z, vals, z, 8, 8, lambda o: device(x, y, zo(o), c))

    def grads(k, top0):
        top, total, target = stats_end(k, st_z, 8, 8)
        fraction = jnp.zeros((1, 128), F32)
        for i in range(8):
            weight = jnp.full((1, 128), sw[i], F32)
            count = jnp.full((1, 128), cnt[i], jnp.int32).astype(F32)
            fraction = jnp.where(row(strm, k) == i, weight / count, fraction)
        mask = row(msk, k).astype(F32)
        scale = mask * fraction
        norm = jnp.exp(top0 - top) / total
        lossbuf[k, c] = jnp.broadcast_to(mask * (top + jnp.log(total) - target), (8, 128))
        send(lossbuf.at[k, c], lossbuf.at[k, c], sem_g.at[k, 2], sib)

        cols = pl.ds(aligned(2 * k + c, 128), 128)

        def tile(i, _):
            rows = pl.ds(aligned(i, 256), 256)
            e = recv[k, rows, :]
            hit = jnp.where(vocab_hit(k, i), 1.0, 0.0)
            grad = scale * (e * norm - hit)
            gt[rows, cols] = grad.astype(BF16)
            g[k, pl.ds(aligned(c, 128), 128), rows] = grad.T.astype(BF16)
            return 0

        lax.fori_loop(0, 4, tile, 0)
        mine = pl.ds(aligned(c, 128), 128)
        send(g.at[k, mine], g.at[k, mine], sem_g.at[k, 0], sib)
        send(gt.at[:, cols], gt.at[:, cols], sem_g.at[k, 1], sib)

    def products(k, lo, n):
        def tile(i, _):
            cols = pl.ds(pl.multiple_of(lo + i * 256, 128), 256)
            out = lax.dot_general(g[k], wv[:, cols], NN, preferred_element_type=F32)
            p[k, :, :, :, cols] = out.astype(BF16).reshape(4, 2, 32, 256)
            return 0

        lax.fori_loop(0, n, tile, 0)

    ca, cb = pl.ds(0, WA), pl.ds(WA, WB)

    def to_owner(k, src, dst, sem, h):
        there = h * 2 + c
        own = jnp.logical_and(there == y, c == k)

        pl.when(own)(pltpu.make_async_copy(src, dst, sem).start)
        send(src, dst, sem, device(x, there, z, k), own)

    def hidden_grad(k):
        other = pl.ds(aligned(1 - c, 128), 128)
        landed(g.at[k, other], sem_g.at[k, 0])
        products(k, 0, 5)
        for o in range(1, 4):
            send(p.at[k, xo(o), :, :, ca], xa.at[k, o - 1], sem_xa.at[k, o - 1],
                 device(xo(o), y, z, c))
        products(k, WA, 5)
        tail = pl.ds(HALF - 128, 128)
        out = lax.dot_general(g[k], wv[:, tail], NN, preferred_element_type=F32)
        p[k, :, :, :, tail] = out.astype(BF16).reshape(4, 2, 32, 128)
        for h in range(2):
            to_owner(k, p.at[k, :, h, :, cb], yb.at[y], sem_yb.at[y], h)

    def a_second(k):
        for o in range(3):
            landed(xa.at[k, o], sem_xa.at[k, o])
        for h in range(2):
            total = p[k, x, h, :, 0:WA].astype(F32)
            for o in range(3):
                total += xa[k, o, h].astype(F32)
            ya_src[k, h] = total.astype(BF16)
            to_owner(k, ya_src.at[k, h], ya.at[y], sem_ya.at[y], h)

    def b_second():
        for o in range(4):
            landed(yb.at[o], sem_yb.at[o])
        for bx in range(4):
            total = yb[0, bx].astype(F32)
            for o in range(1, 4):
                total += yb[o, bx].astype(F32)
            xb_src[bx] = total.astype(BF16)
        for o in range(1, 4):
            send(xb_src.at[xo(o)], xb.at[o - 1], sem_xb.at[o - 1], device(xo(o), y, z, c))

    def last():
        for o in range(4):
            landed(ya.at[o], sem_ya.at[o])
        total = ya[0].astype(F32)
        for o in range(1, 4):
            total += ya[o].astype(F32)
        fin[:, 0:WA] = total
        for o in range(3):
            landed(xb.at[o], sem_xb.at[o])
        total = xb_src[x].astype(F32)
        for o in range(3):
            total += xb[o].astype(F32)
        fin[:, WA:HALF] = total
        for i in range(8):
            lo = i * FW // 128 * 128
            wide = min(512, HALF - lo)
            window = fin[:, lo:lo + wide]
            shift = i * FW - lo
            if shift:
                window = pltpu.roll(window, wide - shift, 1)
            zs[i] = window[:, :384].astype(BF16)
        for o in range(1, 8):
            send(zs.at[zo(o)], zr.at[o - 1], sem_z.at[o - 1], device(x, y, zo(o), c))

    def end():
        total = zs[z].astype(F32)
        for o in range(7):
            landed(zr.at[o], sem_z.at[o])
            total += zr[o].astype(F32)
        gh[...] = total[:, :FW].astype(BF16)
        mine = lossbuf[c, x // 2]
        mine = pltpu.roll(mine, (128 - (x % 2) * 64 - yh * 32) % 128, 1)
        loss[...] = mine[0:1, 0:32]

    def head_out(i):
        cols = pl.ds(aligned(i, 256), 256)
        return pltpu.make_async_copy(gws.at[:, cols], gw.at[:, cols], sem_out.at[i])

    def head_grad():
        for k in range(2):
            other = pl.ds(aligned(2 * k + 1 - c, 128), 128)
            landed(gt.at[:, other], sem_g.at[k, 1])
            landed(lossbuf.at[k, 1 - c], sem_g.at[k, 2])

        def tile(i, _):
            cols = pl.ds(aligned(i, 256), 256)
            out = lax.dot_general(gt[:, 0:256], hf[0, :, cols], NN, preferred_element_type=F32)
            out += lax.dot_general(gt[:, 256:512], hf[1, :, cols], NN, preferred_element_type=F32)
            gws[:, cols] = out.astype(BF16)
            head_out(i).start()
            return 0

        lax.fori_loop(0, 10, tile, 0)
        cols = pl.ds(2560, 128)
        out = lax.dot_general(gt[:, 0:256], hf[0, :, cols], NN, preferred_element_type=F32)
        out += lax.dot_general(gt[:, 256:512], hf[1, :, cols], NN, preferred_element_type=F32)
        gws[:, cols] = out.astype(BF16)
        pltpu.make_async_copy(gws.at[:, cols], gw.at[:, cols], sem_out.at[10]).start()

    def head_end():
        def tile(i, _):
            head_out(i).wait()
            return 0

        lax.fori_loop(0, 10, tile, 0)
        cols = pl.ds(2560, 128)
        pltpu.make_async_copy(gws.at[:, cols], gw.at[:, cols], sem_out.at[10]).wait()

    gather_start(0)
    gather_x(0)
    gather_start(1)
    gather_y(0)
    gather_x(1)
    gather_end(0)
    wcopy.wait()
    logits(0)
    gather_y(1)
    vals0 = local_stats(0)
    stats_x(0, vals0)
    gather_end(1)
    logits(1)
    stats_y(0)
    vals1 = local_stats(1)
    stats_x(1, vals1)
    stats_z(0)
    stats_y(1)
    grads(0, vals0[0])
    stats_z(1)
    hidden_grad(0)
    grads(1, vals1[0])
    a_second(0)
    hidden_grad(1)
    a_second(1)
    b_second()
    head_grad()
    last()
    end()
    head_end()
    for cp, unless in sends:
        if unless is None:
            cp.wait_send()
        else:
            pl.when(jnp.logical_not(unless))(cp.wait_send)


def on_device(hidden, weight, targets, streams, loss_token_mask, counts, stream_weight):
    vm = pl.BlockSpec(memory_space=pltpu.VMEM)
    sm = pl.BlockSpec(memory_space=pltpu.SMEM)
    hbm = pl.BlockSpec(memory_space=pl.ANY)
    dma = pltpu.SemaphoreType.DMA
    rows = lambda a: a.reshape(4, 128)
    gh, gw, loss = pl.pallas_call(
        kernel,
        out_shape=(
            jax.ShapeDtypeStruct((32, FW), BF16),
            jax.ShapeDtypeStruct((V, HALF), BF16),
            jax.ShapeDtypeStruct((1, 32), F32),
        ),
        in_specs=[hbm, hbm, vm, vm, vm, sm, sm],
        out_specs=(vm, hbm, vm),
        scratch_shapes=[
            pltpu.VMEM((V, HALF), BF16),
            pltpu.VMEM((2, 256, HALF), BF16),
            pltpu.VMEM((2, 2, V, 128), F32),
            pltpu.VMEM((2, V, 128), F32),
            pltpu.VMEM((2, 4, 8, 128), F32),
            pltpu.VMEM((2, 4, 8, 128), F32),
            pltpu.VMEM((2, 8, 8, 128), F32),
            pltpu.VMEM((V, 512), BF16),
            pltpu.VMEM((2, 256, V), BF16),
            pltpu.VMEM((2, 4, 2, 32, HALF), BF16),
            pltpu.VMEM((V, HALF), BF16),
            pltpu.VMEM((2, 2, 8, 128), F32),
            pltpu.VMEM((2, 3, 2, 32, WA), BF16),
            pltpu.VMEM((2, 2, 32, WA), BF16),
            pltpu.VMEM((4, 32, WA), BF16),
            pltpu.VMEM((4, 4, 32, WB), BF16),
            pltpu.VMEM((4, 32, WB), BF16),
            pltpu.VMEM((3, 32, WB), BF16),
            pltpu.VMEM((32, HALF), F32),
            pltpu.VMEM((8, 32, 384), BF16),
            pltpu.VMEM((7, 32, 384), BF16),
            dma, dma((11,)), dma((128,)), dma((2,)), dma((2, 2)), dma((2, 2)), dma((2, 4)),
            dma((2, 4)), dma((2,)), dma((2, 16)), dma((2, 3)),
            dma((2, 3)), dma((4,)), dma((4,)), dma((3,)), dma((7,)),
        ],
        compiler_params=pltpu.CompilerParams(
            collective_id=0, has_side_effects=True, vmem_limit_bytes=56 << 20
        ),
        name="head",
    )(hidden, weight, rows(targets), rows(streams), rows(loss_token_mask), counts, stream_weight)
    return gh, gw, loss.reshape(32)


def solution(mesh):
    in_specs = (P(("dp", "seq"), None), P(("seq", "tensor"), "dp"), P(), P(), P(), P(), P())
    out_specs = (P(("dp", "seq"), "tensor"), P(("seq", "tensor"), "dp"), P(("dp", "seq")))
    return jax.shard_map(
        on_device, mesh=mesh, in_specs=in_specs, out_specs=out_specs, check_vma=False
    )
```

```python
import functools

import jax
import jax.numpy as jnp
from jax import lax
from jax.experimental import pallas as pl
from jax.experimental.pallas import tpu as pltpu
from jax.sharding import PartitionSpec as P

MESH = pl.DeviceIdType.MESH
F32, BF16 = jnp.float32, jnp.bfloat16
V, D, HALF = 1024, 5376, 2688
WA = 1280
WB = HALF - WA
FW = 336
NN = (((1,), (0,)), ((), ()))
NT = (((1,), (1,)), ((), ()))


def device(x, y, z, c):
    return (c, x * 2 + y // 2, (y % 2) * 8 + z)


def aligned(index, unit):
    return pl.multiple_of(index * unit, unit)


def landed(ref, sem):
    pltpu.make_async_copy(ref, ref, sem).wait()


def merge(tiles):
    top = functools.reduce(jnp.maximum, [t[0:1] for t in tiles])
    total = sum(t[1:2] * jnp.exp(t[0:1] - top) for t in tiles)
    target = sum(t[2:3] for t in tiles)
    return top, total, target


def kernel(
    hid, w, tgt, strm, msk, cnt, sw,
    gh, gw, loss,
    wv, hf, hs, lg, st_x, st_y, st_z, gt, g, p, lossbuf,
    xa, ya_src, ya, yb, xb_src, xb, fin, zs, zr,
    sem_w, sem_send, sem_own, sem_x, sem_c, sem_p, sem_st, sem_g,
    sem_xa, sem_ya, sem_yb, sem_xb, sem_z,
):
    c, s, t = lax.axis_index("dp"), lax.axis_index("seq"), lax.axis_index("tensor")
    x, yh, yl, z = s // 2, s % 2, t // 8, t % 8
    y = yh * 2 + yl
    sib = device(x, y, z, 1 - c)
    xo = lambda o: (x + o) % 4
    yo = lambda o: (y + o) % 4
    zo = lambda o: (z + o) % 8
    cross = device(x, 3 - y, z, c)
    sends = []

    def send(src, dst, rsem, dev, unless=None):
        cp = pltpu.make_async_remote_copy(
            src_ref=src, dst_ref=dst, send_sem=sem_send.at[len(sends)], recv_sem=rsem,
            device_id=dev, device_id_type=MESH,
        )
        sends.append((cp, unless))
        if unless is None:
            cp.start()
        else:
            pl.when(jnp.logical_not(unless))(cp.start)

    half = z % 2

    def blk(h, bx, by, r0=0, n=32):
        return hf.at[h, pl.ds(pl.multiple_of((bx * 2 + by) * 32 + r0, 16), n), :]

    own = [
        pltpu.make_async_copy(hid.at[:, pl.ds(h * HALF, HALF)], blk(h, x, yh), sem_own.at[h])
        for h in range(2)
    ]
    for cp in own:
        cp.start()
    wcopy = pltpu.make_async_copy(w, wv.at[c], sem_w.at[0])
    wcopy.start()

    barrier = pltpu.get_barrier_semaphore()
    peers = [sib] + [device(x, y, zo(o), c) for o in range(1, 8)]
    for o in range(1, 4):
        peers += [device(xo(o), y, z, c), device(x, yo(o), z, c)]
    for peer in peers:
        pl.semaphore_signal(barrier, inc=1, device_id=peer, device_id_type=MESH)
    pl.semaphore_wait(barrier, len(peers))

    def cross_send(o):
        ref = blk(half, xo(o), yh)
        send(ref, ref, sem_c.at[o], cross)

    def z_send(o, by, base):
        for r in range(2):
            ref = blk(half, xo(o), by, r * 16, 16)
            send(ref, ref, sem_p.at[base + o, r], device(x, y, zo(1 if r == 0 else 7), c))

    def gather_start():
        mine = hid.at[:, pl.ds(aligned(half, HALF), HALF)]
        for o in (1, 3, 2):
            send(mine, blk(half, x, yh), sem_x.at[o - 1], device(xo(o), y, z, c))
        send(mine, blk(half, x, yh), sem_c.at[0], cross)
        send(w, wv.at[c], sem_w.at[1], sib)

    def gather_x(offsets):
        for o in offsets:
            landed(blk(half, xo(o), yh), sem_x.at[3 - o])
            cross_send(o)
            z_send(o, yh, 0)

    def gather_y(offsets):
        for o in offsets:
            landed(blk(half, xo(o), 1 - yh), sem_c.at[o])
            z_send(o, 1 - yh, 4)

    def gather_end():
        for r in range(2):
            for o in range(1, 4):
                landed(blk(1 - half, xo(o), yh, r * 16, 16), sem_p.at[o, r])
            for o in range(4):
                landed(blk(1 - half, xo(o), 1 - yh, r * 16, 16), sem_p.at[4 + o, r])
        for cp in own:
            cp.wait()
        wcopy.wait()
        landed(wv.at[1 - c], sem_w.at[1])

    def logits():
        def tile(i, _):
            rows = pl.ds(aligned(i, 512), 512)
            out = lax.dot_general(wv[0, rows, :], hf[0], NT, preferred_element_type=F32)
            out += lax.dot_general(wv[1, rows, :], hf[1], NT, preferred_element_type=F32)
            lg[rows, :] = out
            return 0

        lax.fori_loop(0, 2, tile, 0)

    def row(ref):
        return jnp.concatenate([ref[pl.ds(2 * c, 1), :], ref[pl.ds(2 * c + 1, 1), :]], axis=1)

    def vocab_hit(i):
        ids = (s * 16 + t) * V + i * 256 + lax.broadcasted_iota(jnp.int32, (256, 256), 0)
        return ids == row(tgt)

    def local_stats():
        def highest(i, top):
            return jnp.maximum(top, jnp.max(lg[pl.ds(aligned(i, 256), 256), :], axis=0, keepdims=True))

        top = lax.fori_loop(0, 4, highest, jnp.full((1, 256), -jnp.inf, F32))

        def expo(i, carry):
            total, target = carry
            rows = pl.ds(aligned(i, 256), 256)
            logit = lg[rows, :]
            e = jnp.exp(logit - top)
            lg[rows, :] = e
            target += jnp.sum(jnp.where(vocab_hit(i), logit, 0.0), axis=0, keepdims=True)
            return total + jnp.sum(e, axis=0, keepdims=True), target

        zero = jnp.zeros((1, 256), F32)
        total, target = lax.fori_loop(0, 4, expo, (zero, zero))
        return top, total, target

    def exchange(buf, vals, n, base, dev):
        buf[0] = jnp.concatenate([*vals, jnp.zeros((5, 256), F32)], axis=0)
        for o in range(1, n):
            send(buf.at[0], buf.at[o], sem_st.at[base + o], dev(o))
        for o in range(1, n):
            landed(buf.at[o], sem_st.at[base + o])
        return merge([buf[o] for o in range(n)])

    def grads():
        vals = local_stats()
        top0 = vals[0]
        vals = exchange(st_x, vals, 4, 0, lambda o: device(xo(o), y, z, c))
        vals = exchange(st_y, vals, 4, 4, lambda o: device(x, yo(o), z, c))
        top, total, target = exchange(st_z, vals, 8, 8, lambda o: device(x, y, zo(o), c))
        fraction = jnp.zeros((1, 256), F32)
        for i in range(8):
            weight = jnp.full((1, 256), sw[i], F32)
            count = jnp.full((1, 256), cnt[i], jnp.int32).astype(F32)
            fraction = jnp.where(row(strm) == i, weight / count, fraction)
        mask = row(msk).astype(F32)
        scale = mask * fraction
        norm = jnp.exp(top0 - top) / total
        row_loss = mask * (top + jnp.log(total) - target)
        for h in range(2):
            lossbuf[h] = jnp.broadcast_to(row_loss[:, h * 128:h * 128 + 128], (8, 128))

        def tile(i, _):
            rows = pl.ds(aligned(i, 256), 256)
            hit = jnp.where(vocab_hit(i), 1.0, 0.0)
            grad = scale * (lg[rows, :] * norm - hit)
            gt[c, rows, :] = grad.astype(BF16)
            g[:, rows] = grad.T.astype(BF16)
            return 0

        lax.fori_loop(0, 4, tile, 0)
        send(gt.at[c], gt.at[c], sem_g.at[0], sib)

    ca, cb = pl.ds(0, WA), pl.ds(WA, WB)

    def products(h, lo, n):
        def tile(i, _):
            cols = pl.ds(pl.multiple_of(lo + i * 256, 128), 256)
            out = lax.dot_general(g[...], wv[h, :, cols], NN, preferred_element_type=F32)
            p[h, :, :, :, cols] = out.astype(BF16).reshape(4, 2, 32, 256)
            return 0

        lax.fori_loop(0, n, tile, 0)

    def a_first(h):
        products(h, 0, 5)
        for o in (2, 1, 3):
            send(p.at[h, xo(o), :, :, ca], xa.at[h, o - 1], sem_xa.at[h, o - 1],
                 device(xo(o), y, z, c))

    def b_first():
        for h in range(2):
            products(h, WA, 5)
            tail = pl.ds(HALF - 128, 128)
            out = lax.dot_general(g[...], wv[h, :, tail], NN, preferred_element_type=F32)
            p[h, :, :, :, tail] = out.astype(BF16).reshape(4, 2, 32, 128)
        for o in (2, 1, 3):
            there = yo(o)
            send(p.at[there % 2, :, there // 2, :, cb], yb.at[o - 1], sem_yb.at[o - 1],
                 device(x, there, z, c))

    def a_second(h):
        for o in range(3):
            landed(xa.at[h, o], sem_xa.at[h, o])
        for k in range(2):
            total = p[h, x, k, :, 0:WA].astype(F32)
            for o in range(3):
                total += xa[h, o, k].astype(F32)
            ya_src[h, k] = total.astype(BF16)
            there = 2 * k + h
            send(ya_src.at[h, k], ya.at[y], sem_ya.at[y], device(x, there, z, c), there == y)

    def b_second():
        for o in range(3):
            landed(yb.at[o], sem_yb.at[o])
        for k in range(4):
            total = p[yl, k, yh, :, WA:HALF].astype(F32)
            for o in range(3):
                total += yb[o, k].astype(F32)
            xb_src[k] = total.astype(BF16)
        for o in (2, 1, 3):
            send(xb_src.at[xo(o)], xb.at[o - 1], sem_xb.at[o - 1], device(xo(o), y, z, c))

    def last():
        total = ya_src[yl, yh].astype(F32)
        for o in range(1, 4):
            landed(ya.at[yo(o)], sem_ya.at[yo(o)])
            total += ya[yo(o)].astype(F32)
        fin[:, 0:WA] = total
        total = xb_src[x].astype(F32)
        for o in range(3):
            landed(xb.at[o], sem_xb.at[o])
            total += xb[o].astype(F32)
        fin[:, WA:HALF] = total
        for i in range(8):
            lo = i * FW // 128 * 128
            wide = min(512, HALF - lo)
            window = fin[:, lo:lo + wide]
            shift = i * FW - lo
            if shift:
                window = pltpu.roll(window, wide - shift, 1)
            zs[i] = window[:, :384].astype(BF16)
        for o in (4, 3, 5, 2, 6, 1, 7):
            send(zs.at[zo(o)], zr.at[o - 1], sem_z.at[o - 1], device(x, y, zo(o), c))

    def end():
        total = zs[z].astype(F32)
        for o in range(7):
            landed(zr.at[o], sem_z.at[o])
            total += zr[o].astype(F32)
        gh[...] = total[:, :FW].astype(BF16)
        row_loss = lossbuf[x // 2]
        row_loss = pltpu.roll(row_loss, (128 - (x % 2) * 64 - yh * 32) % 128, 1)
        loss[...] = row_loss[0:1, 0:32]

    def head_tile(cols):
        out = lax.dot_general(gt[c], hf[c, :, cols], NN, preferred_element_type=F32)
        out += lax.dot_general(gt[1 - c], hs[:, cols], NN, preferred_element_type=F32)
        gw[:, cols] = out.astype(BF16)

    def head_grad():
        landed(gt.at[1 - c], sem_g.at[0])
        landed(hs, sem_g.at[1])

        def tile(i, _):
            head_tile(pl.ds(aligned(i, 256), 256))
            return 0

        lax.fori_loop(0, 10, tile, 0)
        head_tile(pl.ds(2560, 128))

    gather_start()
    gather_x((1, 3))
    gather_y((0,))
    gather_x((2,))
    gather_y((1, 3, 2))
    gather_end()
    logits()
    send(hf.at[1 - c], hs, sem_g.at[1], sib)
    grads()
    a_first(0)
    b_first()
    a_first(1)
    head_grad()
    a_second(0)
    a_second(1)
    b_second()
    last()
    end()
    for cp, unless in sends:
        if unless is None:
            cp.wait_send()
        else:
            pl.when(jnp.logical_not(unless))(cp.wait_send)


def on_device(hidden, weight, targets, streams, loss_token_mask, counts, stream_weight):
    vm = pl.BlockSpec(memory_space=pltpu.VMEM)
    sm = pl.BlockSpec(memory_space=pltpu.SMEM)
    hbm = pl.BlockSpec(memory_space=pl.ANY)
    dma = pltpu.SemaphoreType.DMA
    rows = lambda a: a.reshape(4, 128)
    outs = (((32, FW), BF16), ((V, HALF), BF16), ((1, 32), F32))
    gh, gw, loss = pl.pallas_call(
        kernel,
        out_shape=tuple(pltpu.VMEM(*out) for out in outs),
        in_specs=[hbm, hbm, vm, vm, vm, sm, sm],
        out_specs=(vm, vm, vm),
        scratch_shapes=[
            pltpu.VMEM((2, V, HALF), BF16),
            pltpu.VMEM((2, 256, HALF), BF16),
            pltpu.VMEM((256, HALF), BF16),
            pltpu.VMEM((V, 256), F32),
            pltpu.VMEM((4, 8, 256), F32),
            pltpu.VMEM((4, 8, 256), F32),
            pltpu.VMEM((8, 8, 256), F32),
            pltpu.VMEM((2, V, 256), BF16),
            pltpu.VMEM((256, V), BF16),
            pltpu.VMEM((2, 4, 2, 32, HALF), BF16),
            pltpu.VMEM((2, 8, 128), F32),
            pltpu.VMEM((2, 3, 2, 32, WA), BF16),
            pltpu.VMEM((2, 2, 32, WA), BF16),
            pltpu.VMEM((4, 32, WA), BF16),
            pltpu.VMEM((3, 4, 32, WB), BF16),
            pltpu.VMEM((4, 32, WB), BF16),
            pltpu.VMEM((3, 32, WB), BF16),
            pltpu.VMEM((32, HALF), F32),
            pltpu.VMEM((8, 32, 384), BF16),
            pltpu.VMEM((7, 32, 384), BF16),
            dma((2,)), dma((96,)), dma((2,)), dma((3,)), dma((4,)), dma((8, 2)), dma((16,)),
            dma((2,)),
            dma((2, 3)), dma((4,)), dma((3,)), dma((3,)), dma((7,)),
        ],
        compiler_params=pltpu.CompilerParams(
            collective_id=0, has_side_effects=True, vmem_limit_bytes=56 << 20
        ),
        name="head",
    )(hidden, weight, rows(targets), rows(streams), rows(loss_token_mask), counts, stream_weight)
    return gh, gw, loss.reshape(32)


def solution(mesh):
    in_specs = (P(("dp", "seq"), None), P(("seq", "tensor"), "dp"), P(), P(), P(), P(), P())
    out_specs = (P(("dp", "seq"), "tensor"), P(("seq", "tensor"), "dp"), P(("dp", "seq")))
    return jax.shard_map(
        on_device, mesh=mesh, in_specs=in_specs, out_specs=out_specs, check_vma=False
    )
```

```python
import functools

import jax
import jax.numpy as jnp
from jax import lax
from jax.experimental import pallas as pl
from jax.experimental.pallas import tpu as pltpu
from jax.sharding import PartitionSpec as P

MESH = pl.DeviceIdType.MESH
F32, BF16 = jnp.float32, jnp.bfloat16
V, D, HALF = 1024, 5376, 2688
WA = 1408
WB = HALF - WA
FW = 336
NN = (((1,), (0,)), ((), ()))
NT = (((1,), (1,)), ((), ()))


def device(x, y, z, c):
    return (c, x * 2 + y // 2, (y % 2) * 8 + z)


def aligned(index, unit):
    return pl.multiple_of(index * unit, unit)


def landed(ref, sem):
    pltpu.make_async_copy(ref, ref, sem).wait()


def merge(tiles):
    top = functools.reduce(jnp.maximum, [t[0:2] for t in tiles])
    total = sum(t[2:4] * jnp.exp(t[0:2] - top) for t in tiles)
    target = sum(t[4:6] for t in tiles)
    return [jnp.concatenate([v[0:1], v[1:2]], axis=1) for v in (top, total, target)]


def kernel(
    hid, w, tgt_in, strm_in, msk_in, cnt_in, sw_in,
    gh, gw, loss,
    tgt, strm, msk, cnt, sw, wv, hf, hs, lg, et, st_x, st_y, st_z, gt, g, p, lossbuf,
    fa, xa, ya_src, ya, fb, yb, xb_src, xb, fin, zs, zr,
    sem_far, sem_in, sem_w, sem_send, sem_own, sem_x, sem_c, sem_q, sem_p, sem_st, sem_g,
    sem_fa, sem_xa, sem_ya, sem_fb, sem_yb, sem_xb, sem_z,
):
    c, s, t = lax.axis_index("dp"), lax.axis_index("seq"), lax.axis_index("tensor")
    x, yh, yl, z = s // 2, s % 2, t // 8, t % 8
    y = yh * 2 + yl
    sib = device(x, y, z, 1 - c)
    xo = lambda o: (x + o) % 4
    yo = lambda o: (y + o) % 4
    zo = lambda o: (z + o) % 8
    cross = device(x, 3 - y, z, c)
    sends = []

    def send(src, dst, rsem, dev, unless=None):
        cp = pltpu.make_async_remote_copy(
            src_ref=src, dst_ref=dst, send_sem=sem_send.at[len(sends)], recv_sem=rsem,
            device_id=dev, device_id_type=MESH,
        )
        sends.append((cp, unless))
        if unless is None:
            cp.start()
        else:
            pl.when(jnp.logical_not(unless))(cp.start)

    half = z % 2

    def blk(h, bx, by, r0=0, n=32):
        return hf.at[h, pl.ds(pl.multiple_of((bx * 2 + by) * 32 + r0, 16), n), :]

    pairs = ((tgt_in, tgt), (strm_in, strm), (msk_in, msk), (cnt_in, cnt), (sw_in, sw))
    own = [pltpu.make_async_copy(a, b, sem_in.at[i]) for i, (a, b) in enumerate(pairs)]
    own += [
        pltpu.make_async_copy(hid.at[:, pl.ds(h * HALF, HALF)], blk(h, x, yh), sem_own.at[h])
        for h in range(2)
    ]
    for cp in own:
        cp.start()
    wcopy = pltpu.make_async_copy(w, wv.at[c], sem_w.at[0])
    wcopy.start()

    barrier = pltpu.get_barrier_semaphore()
    near_z = [device(x, y, zo(o), c) for o in (1, 7)]
    near_y = [device(x, yo(o), z, c) for o in (1, 3)]

    def tell(sem, peers):
        for peer in peers:
            pl.semaphore_signal(sem, inc=1, device_id=peer, device_id_type=MESH)

    tell(barrier, [sib] + [device(xo(o), y, z, c) for o in range(1, 4)] + near_y + near_z)
    pl.semaphore_wait(barrier, 8)
    tell(sem_far.at[0], near_y + near_z)

    def heard(i):
        pl.semaphore_wait(sem_far.at[i], 2 if i else 4)
        if i < 2:
            tell(sem_far.at[i + 1], near_z)

    partner = device(x, yh * 2 + 1 - yl, z, c)

    def z_send(ref, slot, r):
        send(ref, ref, sem_p.at[slot, r], device(x, y, zo(1 + 6 * r), c))

    def gather_start():
        mine = hid.at[:, pl.ds(aligned(half, HALF), HALF)]
        for o in (1, 3, 2):
            send(mine, blk(half, x, yh), sem_x.at[o - 1], device(xo(o), y, z, c))
        rows = pl.ds(aligned(1 - yl, 16), 16)
        part = hid.at[rows, pl.ds(aligned(half, HALF), HALF)]
        send(part, blk(half, x, yh, (1 - yl) * 16, 16), sem_c.at[0], cross)
        send(w, wv.at[c], sem_w.at[1], sib)

    def gather_x(o):
        landed(blk(half, xo(o), yh), sem_x.at[3 - o])
        ref = blk(half, xo(o), yh) if o == 2 else blk(half, xo(o), yh, (1 - yl) * 16, 16)
        send(ref, ref, sem_c.at[o], cross)
        for r in range(2):
            z_send(blk(half, xo(o), yh, r * 16, 16), o, r)

    def gather_y(o):
        if o == 2:
            landed(blk(half, xo(o), 1 - yh), sem_c.at[o])
            for r in range(2):
                z_send(blk(half, xo(o), 1 - yh, r * 16, 16), 4 + o, r)
        else:
            ref = blk(half, xo(o), 1 - yh, yl * 16, 16)
            landed(ref, sem_c.at[o])
            send(ref, ref, sem_q.at[o], partner)
            z_send(ref, 4 + o, yl)

    def gather_partner(o):
        ref = blk(half, xo(o), 1 - yh, (1 - yl) * 16, 16)
        landed(ref, sem_q.at[o])
        z_send(ref, 4 + o, 1 - yl)

    def gather_end():
        for r in range(2):
            for o in range(1, 4):
                landed(blk(1 - half, xo(o), yh, r * 16, 16), sem_p.at[o, r])
            for o in range(4):
                landed(blk(1 - half, xo(o), 1 - yh, r * 16, 16), sem_p.at[4 + o, r])

    def gather_local():
        for cp in own:
            cp.wait()
        wcopy.wait()
        landed(wv.at[1 - c], sem_w.at[1])

    def logits(h, add=False):
        def tile(i, _):
            rows = pl.ds(aligned(i, 512), 512)
            out = lax.dot_general(wv[h, rows, :], hf[h], NT, preferred_element_type=F32)
            lg[rows, :] = lg[rows, :] + out if add else out
            return 0

        lax.fori_loop(0, 2, tile, 0)

    def row(ref):
        return jnp.concatenate([ref[pl.ds(2 * c, 1), :], ref[pl.ds(2 * c + 1, 1), :]], axis=1)

    def vocab_hit(i):
        ids = (s * 16 + t) * V + i * 256 + lax.broadcasted_iota(jnp.int32, (256, 256), 0)
        return ids == row(tgt)

    def local_stats():
        def highest(i, top):
            return jnp.maximum(top, jnp.max(lg[pl.ds(aligned(i, 256), 256), :], axis=0, keepdims=True))

        top = lax.fori_loop(0, 4, highest, jnp.full((1, 256), -jnp.inf, F32))

        def expo(i, carry):
            total, target = carry
            rows = pl.ds(aligned(i, 256), 256)
            logit = lg[rows, :]
            e = jnp.exp(logit - top)
            lg[rows, :] = e
            target += jnp.sum(jnp.where(vocab_hit(i), logit, 0.0), axis=0, keepdims=True)
            return total + jnp.sum(e, axis=0, keepdims=True), target

        zero = jnp.zeros((1, 256), F32)
        total, target = lax.fori_loop(0, 4, expo, (zero, zero))
        return top, total, target

    def exchange(buf, vals, n, base, dev, meanwhile=None):
        rows = [v[:, i * 128:i * 128 + 128] for v in vals for i in range(2)]
        buf[0] = jnp.concatenate([*rows, jnp.zeros((2, 128), F32)], axis=0)
        for o in sorted(range(1, n), key=lambda o: -min(o, n - o)):
            send(buf.at[0], buf.at[o], sem_st.at[base + o], dev(o))
        if meanwhile is not None:
            meanwhile()
        for o in range(1, n):
            landed(buf.at[o], sem_st.at[base + o])
        return merge([buf[o] for o in range(n)])

    def turn():
        def tile(i, _):
            rows = pl.ds(aligned(i, 256), 256)
            et[:, rows] = lg[rows, :].T
            return 0

        lax.fori_loop(0, 4, tile, 0)

    def grads():
        vals = local_stats()
        top0 = vals[0]
        vals = exchange(st_x, vals, 4, 0, lambda o: device(xo(o), y, z, c), turn)
        vals = exchange(st_y, vals, 4, 4, lambda o: device(x, yo(o), z, c))
        fraction = jnp.zeros((1, 256), F32)
        for i in range(8):
            weight = jnp.full((1, 256), sw[i], F32)
            count = jnp.full((1, 256), cnt[i], jnp.int32).astype(F32)
            fraction = jnp.where(row(strm) == i, weight / count, fraction)
        mask = row(msk).astype(F32)
        scale = mask * fraction
        top, total, target = exchange(st_z, vals, 8, 8, lambda o: device(x, y, zo(o), c))
        norm = jnp.exp(top0 - top) / total
        stack = [norm, scale, row(tgt).astype(F32), jnp.zeros((5, 256), F32)]
        columns = jnp.concatenate(stack, axis=0).T
        norm_c, scale_c, target_c = columns[:, 0:1], columns[:, 1:2], columns[:, 2:3]
        first_id = ((s * 16 + t) * V).astype(F32)

        def tile(i, _):
            cols = pl.ds(aligned(i, 256), 256)
            place = i * 256 + lax.broadcasted_iota(jnp.int32, (256, 256), 1)
            hit = jnp.where(place.astype(F32) + first_id == target_c, 1.0, 0.0)
            g[:, cols] = (scale_c * (et[:, cols] * norm_c - hit)).astype(BF16)
            return 0

        lax.fori_loop(0, 4, tile, 0)
        row_loss = mask * (top + jnp.log(total) - target)
        for h in range(2):
            lossbuf[h] = jnp.broadcast_to(row_loss[:, h * 128:h * 128 + 128], (8, 128))
        return norm, scale

    def grads_turned(norm, scale):
        def tile(i, _):
            rows = pl.ds(aligned(i, 256), 256)
            hit = jnp.where(vocab_hit(i), 1.0, 0.0)
            gt[c, rows, :] = (scale * (lg[rows, :] * norm - hit)).astype(BF16)
            return 0

        lax.fori_loop(0, 4, tile, 0)
        send(gt.at[c], gt.at[c], sem_g.at[0], sib)

    ca, cb = pl.ds(0, WA), pl.ds(WA, WB)

    def products(h, lo, n):
        def columns(cols, width):
            out = lax.dot_general(g[...], wv[h, :, cols], NN, preferred_element_type=F32)
            p[h, :, :, :, cols] = out.astype(BF16).reshape(4, 2, 32, width)

        def tile(i, _):
            columns(pl.ds(pl.multiple_of(lo + i * 256, 128), 256), 256)
            return 0

        lax.fori_loop(0, n // 256, tile, 0)
        if n % 256:
            columns(pl.ds(lo + n // 256 * 256, n % 256), n % 256)

    def a_first(h):
        products(h, 0, WA)
        for j, o in enumerate((1, 3)):
            dev = device(xo(o), y, z, c)
            send(p.at[h, xo(2), j, :, ca], fa.at[h, j], sem_fa.at[h, j], dev)
            send(p.at[h, xo(o), 1 - j, :, ca], xa.at[h, j, 1 - j], sem_xa.at[h, j, 1 - j], dev)

    def a_mid(h):
        for j, o in enumerate((1, 3)):
            landed(fa.at[h, j], sem_fa.at[h, j])
            both = p[h, xo(o), j, :, 0:WA].astype(F32) + fa[h, j].astype(F32)
            p[h, xo(o), j, :, 0:WA] = both.astype(BF16)
            send(p.at[h, xo(o), j, :, ca], xa.at[h, j, j], sem_xa.at[h, j, j],
                 device(xo(o), y, z, c))

    def a_second(h):
        for k in range(2):
            total = p[h, x, k, :, 0:WA].astype(F32)
            for j in range(2):
                landed(xa.at[h, j, k], sem_xa.at[h, j, k])
                total += xa[h, j, k].astype(F32)
            ya_src[h, k] = total.astype(BF16)
            there = 2 * k + h
            send(ya_src.at[h, k], ya.at[y], sem_ya.at[y], device(x, there, z, c), there == y)

    def piece(there, j):
        return p.at[there % 2, pl.ds(2 * j, 2), there // 2, :, cb]

    def b_first():
        products(yl, WA, WB)
        for j, o in enumerate((1, 3)):
            send(piece(yo(2), j), fb.at[j], sem_fb.at[j], device(x, yo(o), z, c))
        products(1 - yl, WA, WB)
        for j, o in enumerate((1, 3)):
            there = yo(o)
            send(piece(there, 1 - j), yb.at[j, 1 - j], sem_yb.at[j, 1 - j],
                 device(x, there, z, c))

    def b_mid():
        for j, o in enumerate((1, 3)):
            there = yo(o)
            landed(fb.at[j], sem_fb.at[j])
            ref = piece(there, j)
            ref[...] = (ref[...].astype(F32) + fb[j].astype(F32)).astype(BF16)
            send(ref, yb.at[j, j], sem_yb.at[j, j], device(x, there, z, c))

    def b_second():
        for k in range(4):
            total = p[yl, k, yh, :, WA:HALF].astype(F32)
            for j in range(2):
                if k % 2 == 0:
                    landed(yb.at[j, k // 2], sem_yb.at[j, k // 2])
                total += yb[j, k // 2, k % 2].astype(F32)
            xb_src[k] = total.astype(BF16)
        for o in (2, 1, 3):
            send(xb_src.at[xo(o)], xb.at[o - 1], sem_xb.at[o - 1], device(xo(o), y, z, c))

    def last():
        total = ya_src[yl, yh].astype(F32)
        for o in range(1, 4):
            landed(ya.at[yo(o)], sem_ya.at[yo(o)])
            total += ya[yo(o)].astype(F32)
        fin[:, 0:WA] = total
        total = xb_src[x].astype(F32)
        for o in range(3):
            landed(xb.at[o], sem_xb.at[o])
            total += xb[o].astype(F32)
        fin[:, WA:HALF] = total
        for i in range(8):
            lo = i * FW // 128 * 128
            wide = min(512, HALF - lo)
            window = fin[:, lo:lo + wide]
            shift = i * FW - lo
            if shift:
                window = pltpu.roll(window, wide - shift, 1)
            zs[i] = window[:, :384].astype(BF16)
        for o in (4, 3, 5, 2, 6, 1, 7):
            send(zs.at[zo(o)], zr.at[o - 1], sem_z.at[o - 1], device(x, y, zo(o), c))

    def end():
        total = zs[z].astype(F32)
        for o in range(7):
            landed(zr.at[o], sem_z.at[o])
            total += zr[o].astype(F32)
        gh[...] = total[:, :FW].astype(BF16)
        row_loss = lossbuf[x // 2]
        row_loss = pltpu.roll(row_loss, (128 - (x % 2) * 64 - yh * 32) % 128, 1)
        loss[...] = row_loss[0:1, 0:32]

    def head_tile(cols):
        out = lax.dot_general(gt[c], hf[c, :, cols], NN, preferred_element_type=F32)
        out += lax.dot_general(gt[1 - c], hs[:, cols], NN, preferred_element_type=F32)
        gw[:, cols] = out.astype(BF16)

    def head_grad(lo, hi):
        if lo == 0:
            landed(gt.at[1 - c], sem_g.at[0])
            landed(hs, sem_g.at[1])

        def tile(i, _):
            head_tile(pl.ds(aligned(i, 256), 256))
            return 0

        lax.fori_loop(lo, hi, tile, 0)
        if hi == 10:
            head_tile(pl.ds(2560, 128))

    gather_start()
    gather_x(1)
    heard(0)
    gather_x(3)
    heard(1)
    gather_y(0)
    gather_partner(0)
    gather_x(2)
    gather_y(1)
    gather_y(3)
    gather_partner(1)
    gather_partner(3)
    gather_y(2)
    heard(2)
    gather_local()
    logits(half)
    gather_end()
    logits(1 - half, True)
    send(hf.at[1 - c], hs, sem_g.at[1], sib)
    norm, scale = grads()
    a_first(0)
    b_first()
    a_first(1)
    a_mid(0)
    grads_turned(norm, scale)
    b_mid()
    a_mid(1)
    head_grad(0, 6)
    a_second(0)
    head_grad(6, 10)
    a_second(1)
    b_second()
    last()
    end()
    for cp, unless in sends:
        if unless is None:
            cp.wait_send()
        else:
            pl.when(jnp.logical_not(unless))(cp.wait_send)


def on_device(hidden, weight, targets, streams, loss_token_mask, counts, stream_weight):
    vm = pl.BlockSpec(memory_space=pltpu.VMEM)
    hbm = pl.BlockSpec(memory_space=pl.ANY)
    dma = pltpu.SemaphoreType.DMA
    rows = lambda a: a.reshape(4, 128)
    outs = (((32, FW), BF16), ((V, HALF), BF16), ((1, 32), F32))
    gh, gw, loss = pl.pallas_call(
        kernel,
        out_shape=tuple(pltpu.VMEM(*out) for out in outs),
        in_specs=[hbm] * 7,
        out_specs=(vm, vm, vm),
        scratch_shapes=[
            pltpu.VMEM((4, 128), jnp.int32),
            pltpu.VMEM((4, 128), jnp.int32),
            pltpu.VMEM((4, 128), jnp.int32),
            pltpu.SMEM((8,), jnp.int32),
            pltpu.SMEM((8,), F32),
            pltpu.VMEM((2, V, HALF), BF16),
            pltpu.VMEM((2, 256, HALF), BF16),
            pltpu.VMEM((256, HALF), BF16),
            pltpu.VMEM((V, 256), F32),
            pltpu.VMEM((256, V), F32),
            pltpu.VMEM((4, 8, 128), F32),
            pltpu.VMEM((4, 8, 128), F32),
            pltpu.VMEM((8, 8, 128), F32),
            pltpu.VMEM((2, V, 256), BF16),
            pltpu.VMEM((256, V), BF16),
            pltpu.VMEM((2, 4, 2, 32, HALF), BF16),
            pltpu.VMEM((2, 8, 128), F32),
            pltpu.VMEM((2, 2, 32, WA), BF16),
            pltpu.VMEM((2, 2, 2, 32, WA), BF16),
            pltpu.VMEM((2, 2, 32, WA), BF16),
            pltpu.VMEM((4, 32, WA), BF16),
            pltpu.VMEM((2, 2, 32, WB), BF16),
            pltpu.VMEM((2, 2, 2, 32, WB), BF16),
            pltpu.VMEM((4, 32, WB), BF16),
            pltpu.VMEM((3, 32, WB), BF16),
            pltpu.VMEM((32, HALF), F32),
            pltpu.VMEM((8, 32, 384), BF16),
            pltpu.VMEM((7, 32, 384), BF16),
            pltpu.SemaphoreType.REGULAR((3,)),
            dma((5,)), dma((2,)), dma((128,)), dma((2,)), dma((3,)), dma((4,)), dma((4,)), dma((8, 2)), dma((16,)),
            dma((2,)),
            dma((2, 2)), dma((2, 2, 2)), dma((4,)), dma((2,)), dma((2, 2)), dma((3,)), dma((7,)),
        ],
        compiler_params=pltpu.CompilerParams(
            collective_id=0, has_side_effects=True, vmem_limit_bytes=56 << 20
        ),
        name="head",
    )(hidden, weight, rows(targets), rows(streams), rows(loss_token_mask), counts, stream_weight)
    return gh, gw, loss.reshape(32)


def solution(mesh):
    in_specs = (P(("dp", "seq"), None), P(("seq", "tensor"), "dp"), P(), P(), P(), P(), P())
    out_specs = (P(("dp", "seq"), "tensor"), P(("seq", "tensor"), "dp"), P(("dp", "seq")))
    return jax.shard_map(
        on_device, mesh=mesh, in_specs=in_specs, out_specs=out_specs, check_vma=False
    )
```

```python
import functools

import jax
import jax.numpy as jnp
from jax import lax
from jax.experimental import pallas as pl
from jax.experimental.pallas import tpu as pltpu
from jax.sharding import PartitionSpec as P

MESH = pl.DeviceIdType.MESH
F32, BF16 = jnp.float32, jnp.bfloat16
V, D, HALF = 1024, 5376, 2688
WA = 1408
WB = HALF - WA
FW = 336
NN = (((1,), (0,)), ((), ()))
NT = (((1,), (1,)), ((), ()))


def device(x, y, z, c):
    return (c, x * 2 + y // 2, (y % 2) * 8 + z)


def aligned(index, unit):
    return pl.multiple_of(index * unit, unit)


def landed(ref, sem):
    pltpu.make_async_copy(ref, ref, sem).wait()


def merge(tiles):
    top = functools.reduce(jnp.maximum, [t[0:2] for t in tiles])
    total = sum(t[2:4] * jnp.exp(t[0:2] - top) for t in tiles)
    target = sum(t[4:6] for t in tiles)
    return [jnp.concatenate([v[0:1], v[1:2]], axis=1) for v in (top, total, target)]


def kernel(
    hid, w, tgt_in, strm_in, msk_in, cnt_in, sw_in,
    gh, gw, loss,
    tgt, strm, msk, cnt, sw, wv, hf, hs, lg, et, st_x, st_y, st_z, gt, g, p, lossbuf,
    fa, xa, ya_src, ya, fb, yb, xb_src, xb, fin, zs, zr,
    sem_far, sem_in, sem_w, sem_send, sem_own, sem_x, sem_c, sem_q, sem_p, sem_st, sem_g,
    sem_fa, sem_xa, sem_ya, sem_fb, sem_yb, sem_xb, sem_z,
):
    c, s, t = lax.axis_index("dp"), lax.axis_index("seq"), lax.axis_index("tensor")
    x, yh, yl, z = s // 2, s % 2, t // 8, t % 8
    y = yh * 2 + yl
    sib = device(x, y, z, 1 - c)
    xo = lambda o: (x + o) % 4
    yo = lambda o: (y + o) % 4
    zo = lambda o: (z + o) % 8
    cross = device(x, 3 - y, z, c)
    sends = []

    def send(src, dst, rsem, dev, unless=None):
        cp = pltpu.make_async_remote_copy(
            src_ref=src, dst_ref=dst, send_sem=sem_send.at[len(sends)], recv_sem=rsem,
            device_id=dev, device_id_type=MESH,
        )
        sends.append((cp, unless))
        if unless is None:
            cp.start()
        else:
            pl.when(jnp.logical_not(unless))(cp.start)

    half = z % 2

    def blk(h, bx, by, r0=0, n=32):
        return hf.at[h, pl.ds(pl.multiple_of((bx * 2 + by) * 32 + r0, 16), n), :]

    pairs = ((tgt_in, tgt), (strm_in, strm), (msk_in, msk), (cnt_in, cnt), (sw_in, sw))
    own = [pltpu.make_async_copy(a, b, sem_in.at[i]) for i, (a, b) in enumerate(pairs)]
    own += [
        pltpu.make_async_copy(hid.at[:, pl.ds(h * HALF, HALF)], blk(h, x, yh), sem_own.at[h])
        for h in range(2)
    ]
    for cp in own:
        cp.start()
    wcopy = pltpu.make_async_copy(w, wv.at[c], sem_w.at[0])
    wcopy.start()

    barrier = pltpu.get_barrier_semaphore()
    near_z = [device(x, y, zo(o), c) for o in (1, 7)]
    near_y = [device(x, yo(o), z, c) for o in (1, 3)]

    def tell(sem, peers):
        for peer in peers:
            pl.semaphore_signal(sem, inc=1, device_id=peer, device_id_type=MESH)

    tell(barrier, [sib] + [device(xo(o), y, z, c) for o in range(1, 4)] + near_y + near_z)
    pl.semaphore_wait(barrier, 8)
    tell(sem_far.at[0], near_y + near_z)

    def heard(i):
        pl.semaphore_wait(sem_far.at[i], 2 if i else 4)
        if i < 2:
            tell(sem_far.at[i + 1], near_z)

    partner = device(x, yh * 2 + 1 - yl, z, c)

    def z_send(ref, slot, r):
        send(ref, ref, sem_p.at[slot, r], device(x, y, zo(1 + 6 * r), c))

    def gather_start():
        mine = hid.at[:, pl.ds(aligned(half, HALF), HALF)]
        for o in (1, 3, 2):
            send(mine, blk(half, x, yh), sem_x.at[o - 1], device(xo(o), y, z, c))
        rows = pl.ds(aligned(1 - yl, 16), 16)
        part = hid.at[rows, pl.ds(aligned(half, HALF), HALF)]
        send(part, blk(half, x, yh, (1 - yl) * 16, 16), sem_c.at[0], cross)
        send(w, wv.at[c], sem_w.at[1], sib)

    def gather_x(o):
        landed(blk(half, xo(o), yh), sem_x.at[3 - o])
        ref = blk(half, xo(o), yh) if o == 2 else blk(half, xo(o), yh, (1 - yl) * 16, 16)
        send(ref, ref, sem_c.at[o], cross)
        for r in range(2):
            z_send(blk(half, xo(o), yh, r * 16, 16), o, r)

    def gather_y(o):
        if o == 2:
            landed(blk(half, xo(o), 1 - yh), sem_c.at[o])
            for r in range(2):
                z_send(blk(half, xo(o), 1 - yh, r * 16, 16), 4 + o, r)
        else:
            ref = blk(half, xo(o), 1 - yh, yl * 16, 16)
            landed(ref, sem_c.at[o])
            send(ref, ref, sem_q.at[o], partner)
            z_send(ref, 4 + o, yl)

    def gather_partner(o):
        ref = blk(half, xo(o), 1 - yh, (1 - yl) * 16, 16)
        landed(ref, sem_q.at[o])
        z_send(ref, 4 + o, 1 - yl)

    def gather_end():
        for r in range(2):
            for o in range(1, 4):
                landed(blk(1 - half, xo(o), yh, r * 16, 16), sem_p.at[o, r])
            for o in range(4):
                landed(blk(1 - half, xo(o), 1 - yh, r * 16, 16), sem_p.at[4 + o, r])

    def gather_local():
        for cp in own:
            cp.wait()
        wcopy.wait()
        landed(wv.at[1 - c], sem_w.at[1])

    def logits(h, add=False):
        def tile(i, _):
            rows = pl.ds(aligned(i, 512), 512)
            out = lax.dot_general(wv[h, rows, :], hf[h], NT, preferred_element_type=F32)
            lg[rows, :] = lg[rows, :] + out if add else out
            return 0

        lax.fori_loop(0, 2, tile, 0)

    def row(ref):
        return jnp.concatenate([ref[pl.ds(2 * c, 1), :], ref[pl.ds(2 * c + 1, 1), :]], axis=1)

    def vocab_hit(i):
        ids = (s * 16 + t) * V + i * 256 + lax.broadcasted_iota(jnp.int32, (256, 256), 0)
        return ids == row(tgt)

    def local_stats():
        def highest(i, top):
            return jnp.maximum(top, jnp.max(lg[pl.ds(aligned(i, 256), 256), :], axis=0, keepdims=True))

        top = lax.fori_loop(0, 4, highest, jnp.full((1, 256), -jnp.inf, F32))

        def expo(i, carry):
            total, target = carry
            rows = pl.ds(aligned(i, 256), 256)
            logit = lg[rows, :]
            e = jnp.exp(logit - top)
            lg[rows, :] = e
            target += jnp.sum(jnp.where(vocab_hit(i), logit, 0.0), axis=0, keepdims=True)
            return total + jnp.sum(e, axis=0, keepdims=True), target

        zero = jnp.zeros((1, 256), F32)
        total, target = lax.fori_loop(0, 4, expo, (zero, zero))
        return top, total, target

    def exchange(buf, vals, n, base, dev, meanwhile=None):
        rows = [v[:, i * 128:i * 128 + 128] for v in vals for i in range(2)]
        buf[0] = jnp.concatenate([*rows, jnp.zeros((2, 128), F32)], axis=0)
        for o in sorted(range(1, n), key=lambda o: -min(o, n - o)):
            send(buf.at[0], buf.at[o], sem_st.at[base + o], dev(o))
        if meanwhile is not None:
            meanwhile()
        for o in range(1, n):
            landed(buf.at[o], sem_st.at[base + o])
        return merge([buf[o] for o in range(n)])

    def turn():
        def tile(i, _):
            rows = pl.ds(aligned(i, 256), 256)
            et[:, rows] = lg[rows, :].T
            return 0

        lax.fori_loop(0, 4, tile, 0)

    def grads():
        vals = local_stats()
        top0 = vals[0]
        vals = exchange(st_x, vals, 4, 0, lambda o: device(xo(o), y, z, c), turn)
        vals = exchange(st_y, vals, 4, 4, lambda o: device(x, yo(o), z, c))
        fraction = jnp.zeros((1, 256), F32)
        for i in range(8):
            weight = jnp.full((1, 256), sw[i], F32)
            count = jnp.full((1, 256), cnt[i], jnp.int32).astype(F32)
            fraction = jnp.where(row(strm) == i, weight / count, fraction)
        mask = row(msk).astype(F32)
        scale = mask * fraction
        top, total, target = exchange(st_z, vals, 8, 8, lambda o: device(x, y, zo(o), c))
        norm = jnp.exp(top0 - top) / total
        stack = [norm, scale, row(tgt).astype(F32), jnp.zeros((5, 256), F32)]
        columns = jnp.concatenate(stack, axis=0).T
        norm_c, scale_c, target_c = columns[:, 0:1], columns[:, 1:2], columns[:, 2:3]
        first_id = ((s * 16 + t) * V).astype(F32)

        def tile(i, _):
            cols = pl.ds(aligned(i, 256), 256)
            place = i * 256 + lax.broadcasted_iota(jnp.int32, (256, 256), 1)
            hit = jnp.where(place.astype(F32) + first_id == target_c, 1.0, 0.0)
            g[:, cols] = (scale_c * (et[:, cols] * norm_c - hit)).astype(BF16)
            return 0

        lax.fori_loop(0, 4, tile, 0)
        row_loss = mask * (top + jnp.log(total) - target)
        for h in range(2):
            lossbuf[h] = jnp.broadcast_to(row_loss[:, h * 128:h * 128 + 128], (8, 128))
        return norm, scale

    def grads_turned(norm, scale):
        def tile(i, _):
            rows = pl.ds(aligned(i, 256), 256)
            hit = jnp.where(vocab_hit(i), 1.0, 0.0)
            gt[c, rows, :] = (scale * (lg[rows, :] * norm - hit)).astype(BF16)
            return 0

        lax.fori_loop(0, 4, tile, 0)
        send(gt.at[c], gt.at[c], sem_g.at[0], sib)

    ca, cb = pl.ds(0, WA), pl.ds(WA, WB)

    def products(h, lo, n):
        def columns(cols, width):
            out = lax.dot_general(g[...], wv[h, :, cols], NN, preferred_element_type=F32)
            p[h, :, :, :, cols] = out.astype(BF16).reshape(4, 2, 32, width)

        def tile(i, _):
            columns(pl.ds(pl.multiple_of(lo + i * 256, 128), 256), 256)
            return 0

        lax.fori_loop(0, n // 256, tile, 0)
        if n % 256:
            columns(pl.ds(lo + n // 256 * 256, n % 256), n % 256)

    def a_first(h):
        products(h, 0, WA)
        for j, o in enumerate((1, 3)):
            dev = device(xo(o), y, z, c)
            send(p.at[h, xo(2), j, :, ca], fa.at[h, j], sem_fa.at[h, j], dev)
            send(p.at[h, xo(o), 1 - j, :, ca], xa.at[h, j, 1 - j], sem_xa.at[h, j, 1 - j], dev)

    def a_mid(h):
        for j, o in enumerate((1, 3)):
            landed(fa.at[h, j], sem_fa.at[h, j])
            both = p[h, xo(o), j, :, 0:WA].astype(F32) + fa[h, j].astype(F32)
            p[h, xo(o), j, :, 0:WA] = both.astype(BF16)
            send(p.at[h, xo(o), j, :, ca], xa.at[h, j, j], sem_xa.at[h, j, j],
                 device(xo(o), y, z, c))

    def a_second(h):
        for k in range(2):
            total = p[h, x, k, :, 0:WA].astype(F32)
            for j in range(2):
                landed(xa.at[h, j, k], sem_xa.at[h, j, k])
                total += xa[h, j, k].astype(F32)
            ya_src[h, k] = total.astype(BF16)
            there = 2 * k + h
            send(ya_src.at[h, k], ya.at[y], sem_ya.at[y], device(x, there, z, c), there == y)

    def piece(there, j):
        return p.at[there % 2, pl.ds(2 * j, 2), there // 2, :, cb]

    def b_first():
        products(yl, WA, WB)
        for j, o in enumerate((1, 3)):
            send(piece(yo(2), j), fb.at[j], sem_fb.at[j], device(x, yo(o), z, c))
        products(1 - yl, WA, WB)
        for j, o in enumerate((1, 3)):
            there = yo(o)
            send(piece(there, 1 - j), yb.at[j, 1 - j], sem_yb.at[j, 1 - j],
                 device(x, there, z, c))

    def b_mid():
        for j, o in enumerate((1, 3)):
            there = yo(o)
            landed(fb.at[j], sem_fb.at[j])
            ref = piece(there, j)
            ref[...] = (ref[...].astype(F32) + fb[j].astype(F32)).astype(BF16)
            send(ref, yb.at[j, j], sem_yb.at[j, j], device(x, there, z, c))

    def b_second():
        for k in range(4):
            total = p[yl, k, yh, :, WA:HALF].astype(F32)
            for j in range(2):
                if k % 2 == 0:
                    landed(yb.at[j, k // 2], sem_yb.at[j, k // 2])
                total += yb[j, k // 2, k % 2].astype(F32)
            xb_src[k] = total.astype(BF16)
        for o in (2, 1, 3):
            send(xb_src.at[xo(o)], xb.at[o - 1], sem_xb.at[o - 1], device(xo(o), y, z, c))

    def last():
        total = ya_src[yl, yh].astype(F32)
        for o in range(1, 4):
            landed(ya.at[yo(o)], sem_ya.at[yo(o)])
            total += ya[yo(o)].astype(F32)
        fin[:, 0:WA] = total
        total = xb_src[x].astype(F32)
        for o in range(3):
            landed(xb.at[o], sem_xb.at[o])
            total += xb[o].astype(F32)
        fin[:, WA:HALF] = total
        for i in range(8):
            lo = i * FW // 128 * 128
            wide = min(512, HALF - lo)
            window = fin[:, lo:lo + wide]
            shift = i * FW - lo
            if shift:
                window = pltpu.roll(window, wide - shift, 1)
            zs[i] = window[:, :384].astype(BF16)
        for o in (4, 3, 5, 2, 6, 1, 7):
            send(zs.at[zo(o)], zr.at[o - 1], sem_z.at[o - 1], device(x, y, zo(o), c))

    def end():
        total = zs[z].astype(F32)
        for o in range(7):
            landed(zr.at[o], sem_z.at[o])
            total += zr[o].astype(F32)
        gh[...] = total[:, :FW].astype(BF16)
        row_loss = lossbuf[x // 2]
        row_loss = pltpu.roll(row_loss, (128 - (x % 2) * 64 - yh * 32) % 128, 1)
        loss[...] = row_loss[0:1, 0:32]

    def head_tile(cols):
        out = lax.dot_general(gt[c], hf[c, :, cols], NN, preferred_element_type=F32)
        out += lax.dot_general(gt[1 - c], hs[:, cols], NN, preferred_element_type=F32)
        gw[:, cols] = out.astype(BF16)

    def head_grad(lo, hi):
        if lo == 0:
            landed(gt.at[1 - c], sem_g.at[0])
            landed(hs, sem_g.at[1])

        def tile(i, _):
            head_tile(pl.ds(aligned(i, 256), 256))
            return 0

        lax.fori_loop(lo, hi, tile, 0)
        if hi == 10:
            head_tile(pl.ds(2560, 128))

    gather_start()
    gather_x(1)
    heard(0)
    gather_x(3)
    heard(1)
    gather_y(0)
    gather_partner(0)
    gather_x(2)
    gather_y(1)
    gather_y(3)
    gather_partner(1)
    gather_partner(3)
    gather_y(2)
    heard(2)
    gather_local()
    logits(half)
    gather_end()
    logits(1 - half, True)
    send(hf.at[1 - c], hs, sem_g.at[1], sib)
    norm, scale = grads()
    a_first(0)
    b_first()
    a_first(1)
    grads_turned(norm, scale)
    a_mid(0)
    b_mid()
    head_grad(0, 2)
    a_mid(1)
    head_grad(2, 6)
    a_second(0)
    head_grad(6, 10)
    a_second(1)
    b_second()
    last()
    end()
    for cp, unless in sends:
        if unless is None:
            cp.wait_send()
        else:
            pl.when(jnp.logical_not(unless))(cp.wait_send)


def on_device(hidden, weight, targets, streams, loss_token_mask, counts, stream_weight):
    vm = pl.BlockSpec(memory_space=pltpu.VMEM)
    hbm = pl.BlockSpec(memory_space=pl.ANY)
    dma = pltpu.SemaphoreType.DMA
    rows = lambda a: a.reshape(4, 128)
    outs = (((32, FW), BF16), ((V, HALF), BF16), ((1, 32), F32))
    gh, gw, loss = pl.pallas_call(
        kernel,
        out_shape=tuple(pltpu.VMEM(*out) for out in outs),
        in_specs=[hbm] * 7,
        out_specs=(vm, vm, vm),
        scratch_shapes=[
            pltpu.VMEM((4, 128), jnp.int32),
            pltpu.VMEM((4, 128), jnp.int32),
            pltpu.VMEM((4, 128), jnp.int32),
            pltpu.SMEM((8,), jnp.int32),
            pltpu.SMEM((8,), F32),
            pltpu.VMEM((2, V, HALF), BF16),
            pltpu.VMEM((2, 256, HALF), BF16),
            pltpu.VMEM((256, HALF), BF16),
            pltpu.VMEM((V, 256), F32),
            pltpu.VMEM((256, V), F32),
            pltpu.VMEM((4, 8, 128), F32),
            pltpu.VMEM((4, 8, 128), F32),
            pltpu.VMEM((8, 8, 128), F32),
            pltpu.VMEM((2, V, 256), BF16),
            pltpu.VMEM((256, V), BF16),
            pltpu.VMEM((2, 4, 2, 32, HALF), BF16),
            pltpu.VMEM((2, 8, 128), F32),
            pltpu.VMEM((2, 2, 32, WA), BF16),
            pltpu.VMEM((2, 2, 2, 32, WA), BF16),
            pltpu.VMEM((2, 2, 32, WA), BF16),
            pltpu.VMEM((4, 32, WA), BF16),
            pltpu.VMEM((2, 2, 32, WB), BF16),
            pltpu.VMEM((2, 2, 2, 32, WB), BF16),
            pltpu.VMEM((4, 32, WB), BF16),
            pltpu.VMEM((3, 32, WB), BF16),
            pltpu.VMEM((32, HALF), F32),
            pltpu.VMEM((8, 32, 384), BF16),
            pltpu.VMEM((7, 32, 384), BF16),
            pltpu.SemaphoreType.REGULAR((3,)),
            dma((5,)), dma((2,)), dma((128,)), dma((2,)), dma((3,)), dma((4,)), dma((4,)), dma((8, 2)), dma((16,)),
            dma((2,)),
            dma((2, 2)), dma((2, 2, 2)), dma((4,)), dma((2,)), dma((2, 2)), dma((3,)), dma((7,)),
        ],
        compiler_params=pltpu.CompilerParams(
            collective_id=0, has_side_effects=True, vmem_limit_bytes=56 << 20
        ),
        name="head",
    )(hidden, weight, rows(targets), rows(streams), rows(loss_token_mask), counts, stream_weight)
    return gh, gw, loss.reshape(32)


def solution(mesh):
    in_specs = (P(("dp", "seq"), None), P(("seq", "tensor"), "dp"), P(), P(), P(), P(), P())
    out_specs = (P(("dp", "seq"), "tensor"), P(("seq", "tensor"), "dp"), P(("dp", "seq")))
    return jax.shard_map(
        on_device, mesh=mesh, in_specs=in_specs, out_specs=out_specs, check_vma=False
    )
```
